256 devices in a mesh: dp: 32 (over x, y, core), seq: 8 (over z).
Axes of the slice: x: 4, y: 4, z: 8, core: 2. Of those that a mesh axis runs over, the one named last changes fastest.
Arguments:
- hidden: bfloat16 [32, 8192, 4096], P('dp', 'seq')
- gain: float32 [4096], replicated, may hold values from 0.25 to 1.75
- seg_start: int32 [32, 256], P('dp'), may hold values from 0 to 8191, as said below
- owner: int32 [32, 256], P('dp'), may hold values from 0 to 7, as said below
- queries: bfloat16 [16384, 4096], P('seq', 'dp')
- positive: int32 [16384], P('seq'), may hold values from 0 to 8191
- logit_scale: float32 [1], replicated, may hold values from 200 to 300
Outputs:
- pooled: bfloat16 [8192, 4096], P(('dp', 'seq'))
- log_prob: float32 [16384], P('seq')
The draws below stay inside these ranges and needn't reach their ends.
Inputs may be any that keep to these rules, and one draw needn't show every extreme that they name: `seg_start`: each row's starts rise strictly, the first is 0, and every passage covers at least 16 positions. `owner`: in every row each index of seq owns exactly 32 passages.
All inputs are finite; a program needn't handle non-finite values.
Results may differ from the reference program's by a relative error of at most 0.0049.
Values may be sent and summed in bfloat16 or wider, within the bound.
No kernel may reach another device: no remote copies, remote signals or barrier semaphores. Data moves between devices by JAX's collectives and lax.ppermute only.
A program may use at most 128 MiB of HBM per device.

```python
import jax
import jax.numpy as jnp
from jax import lax

D = 4096
SEGS = 256
QB = 2048
ROW_LEN = 8192
SEG_DEV = 32
QUERIES = 16384
N_DP = 32
N_SEQ = 8


def draw_hidden(key, part):
    key = jax.random.fold_in(key, 1)
    first = jax.random.fold_in(key, 0)
    values = jax.random.normal(first, (N_DP, ROW_LEN, D), jnp.float32)
    return values.astype(jnp.bfloat16)


def draw_queries(key, part):
    key = jax.random.fold_in(key, 2)
    first = jax.random.fold_in(key, 0)
    values = jax.random.normal(first, (QB * N_SEQ, D), jnp.float32)
    return values.astype(jnp.bfloat16)


def draw_seg_start(key, part):
    key = jax.random.fold_in(key, 3)
    keys = jax.random.split(key, N_DP)
    min_gap = min(16, ROW_LEN // (2 * SEGS))
    spread = ROW_LEN - min_gap - (min_gap - 1) * (SEGS - 1)
    offsets = (min_gap - 1) * jnp.arange(1, SEGS, dtype=jnp.int32)

    def one_row(row_key):
        picks = jax.random.permutation(row_key, spread)[:SEGS - 1] + 1
        rest = jnp.sort(picks).astype(jnp.int32) + offsets
        return jnp.concatenate([jnp.zeros((1,), jnp.int32), rest])
    return jax.vmap(one_row)(keys)


def draw_owner(key, part):
    key = jax.random.fold_in(key, 4)
    keys = jax.random.split(key, N_DP)

    def one_row(row_key):
        return (jax.random.permutation(row_key, SEGS) // SEG_DEV).astype(jnp.int32)
    return jax.vmap(one_row)(keys)


def plant(drawn, stream_key, low, high):
    shape = drawn.shape
    index_at = [jax.random.randint(jax.random.fold_in(stream_key, axis), (), 0, shape[axis]) for axis in range(len(shape))]
    drawn = drawn.at[tuple(index_at)].set(low)
    longest = shape.index(max(shape))
    index_at[longest] = (index_at[longest] + 1) % shape[longest]
    return drawn.at[tuple(index_at)].set(high)


def setup_inputs(seed: int = 0) -> dict:
    streams_of = jax.random.split(jax.random.key(seed), 8)
    hidden = draw_hidden(jax.random.fold_in(streams_of[7], 71), 0)
    gain = jnp.clip(1.0 + 0.15 * jax.random.normal(streams_of[1], (D,), jnp.float32), 0.25, 1.75)
    seg_start = draw_seg_start(jax.random.fold_in(streams_of[7], 71), 0)
    owner = draw_owner(jax.random.fold_in(streams_of[7], 71), 0)
    queries = draw_queries(jax.random.fold_in(streams_of[7], 71), 0)
    positive = plant(jax.random.randint(streams_of[5], (QUERIES,), 0, N_DP * SEGS), jax.random.fold_in(streams_of[5], 1), 0, (N_DP * SEGS) - 1).astype(jnp.int32)
    logit_scale = jnp.clip(jax.random.uniform(streams_of[6], (1,), jnp.float32, 200.0, 300.0), 200.0, 300.0)
    return {"hidden": hidden, "gain": gain, "seg_start": seg_start, "owner": owner, "queries": queries, "positive": positive, "logit_scale": logit_scale}


def slot_of(own):
    table = (own[:, None] == jnp.arange(N_SEQ, dtype=jnp.int32)[None, :]).astype(jnp.int32)
    ranked = lax.optimization_barrier(jnp.sum((jnp.cumsum(table, axis=0) - 1) * table, axis=1))
    return (own * (SEGS // N_SEQ) + ranked).astype(jnp.int32)

def reference(hidden, gain, seg_start, owner, queries, positive, logit_scale):
    places = jnp.arange(ROW_LEN, dtype=jnp.int32)

    def pool_row(items):
        states, starts, own = items
        wide = states.astype(jnp.float32)
        meansq = lax.optimization_barrier(jnp.mean(wide * wide, axis=-1, keepdims=True))
        normed = (wide * lax.rsqrt(meansq + 1e-05) * gain).astype(jnp.bfloat16)
        ends = jnp.concatenate([starts[1:], jnp.full((1,), ROW_LEN, jnp.int32)])
        member = lax.optimization_barrier(jnp.sum((starts[None, :] <= places[:, None]).astype(jnp.int32), axis=1)) - 1
        sums = jax.ops.segment_sum(normed.astype(jnp.float32), member, num_segments=SEGS)
        counts = (ends - starts).astype(jnp.float32)
        mean = sums / counts[:, None]
        embed = (mean * lax.rsqrt(lax.optimization_barrier(jnp.sum(mean * mean, axis=1, keepdims=True)) + 1e-06)).astype(jnp.bfloat16)
        ordered = jnp.zeros_like(embed).at[slot_of(own)].set(embed)
        return (embed, ordered)
    embeds, ordered = lax.map(pool_row, (hidden, seg_start, owner))
    pooled = ordered.reshape(N_DP * SEGS, D)
    passages = embeds.reshape(N_DP * SEGS, D)

    def score_block(items):
        block, picks = items
        wide = block.astype(jnp.float32)
        squares = lax.optimization_barrier(jnp.sum(wide * wide, axis=1))
        factor = logit_scale[0] * lax.rsqrt(squares + 1e-06)
        scores = jnp.dot(block, passages.T, preferred_element_type=jnp.float32) * factor[:, None]
        top = lax.optimization_barrier(jnp.max(scores, axis=1))
        total = lax.optimization_barrier(jnp.sum(jnp.exp(scores - top[:, None]), axis=1))
        chosen = jnp.take_along_axis(scores, picks[:, None].astype(jnp.int32), axis=1)[:, 0]
        return chosen - top - jnp.log(total)
    log_prob = lax.map(score_block, (queries.reshape(N_SEQ, QB, D), positive.reshape(N_SEQ, QB)))
    return (pooled, log_prob.reshape(N_SEQ * QB))
```

```python
import jax
import jax.numpy as jnp
from jax import lax
from jax.experimental import pallas as pl
from jax.experimental.pallas import tpu as pltpu
from jax.sharding import PartitionSpec as P

NX, NY, NC = 4, 4, 2
HALF_ROWS = 272
BF = jnp.bfloat16
F32 = jnp.float32
barrier = lax.optimization_barrier


def move(value, dx=0, dy=0, dc=0):
    pairs = []
    for x in range(NX):
        for y in range(NY):
            for c in range(NC):
                to = (((x + dx) % NX) * NY + (y + dy) % NY) * NC + (c + dc) % NC
                pairs.append(((x * NY + y) * NC + c, to))
    return lax.ppermute(value, "dp", pairs)


def turn(value, step):
    n = lax.axis_size("seq")
    return lax.ppermute(value, "seq", [(i, (i + step) % n) for i in range(n)])


def pool_kernel(place, starts, hidden, gain, out, acc):
    step = pl.program_id(0)
    rows = hidden.shape[0]

    @pl.when(step == 0)
    def _():
        acc[...] = jnp.zeros_like(acc)

    wide = hidden[...].astype(F32)
    meansq = jnp.mean(wide * wide, axis=1, keepdims=True)
    normed = (wide * lax.rsqrt(meansq + 1e-05) * gain[...]).astype(BF)
    first = place[0]
    pos = first + step * rows + lax.broadcasted_iota(jnp.int32, (rows, 1), 0)
    begun = (starts[...] <= pos).astype(jnp.int32)
    before = (starts[...] <= first).astype(jnp.int32)
    rel = jnp.sum(begun, axis=1, keepdims=True) - jnp.sum(before, axis=1, keepdims=True)
    lane = lax.broadcasted_iota(jnp.int32, (rows, 128), 1)
    member = (rel == lane).astype(F32).astype(BF)
    acc[...] += lax.dot_general(
        member, normed, (((0,), (0,)), ((), ())), preferred_element_type=F32
    )

    @pl.when(step == pl.num_programs(0) - 1)
    def _():
        for g in range(8):
            out[pl.ds(64 * g, 64), :] = acc[0:64, 512 * g : 512 * g + 512].astype(BF)
        tail = [acc[64:65, 512 * g : 512 * g + 512] for g in range(8)]
        tail.append(jnp.zeros((8, 512), F32))
        out[pl.ds(512, 16), :] = jnp.concatenate(tail, axis=0).astype(BF)


def pool(place, starts, hidden, gain):
    toks, d = hidden.shape
    blk = 256
    return pl.pallas_call(
        pool_kernel,
        out_shape=jax.ShapeDtypeStruct((528, 512), BF),
        grid_spec=pltpu.PrefetchScalarGridSpec(
            num_scalar_prefetch=1,
            grid=(toks // blk,),
            in_specs=[
                pl.BlockSpec((1, 256), lambda i, p: (0, 0)),
                pl.BlockSpec((blk, d), lambda i, p: (i, 0)),
                pl.BlockSpec((1, d), lambda i, p: (0, 0)),
            ],
            out_specs=pl.BlockSpec((528, 512), lambda i, p: (0, 0)),
            scratch_shapes=[pltpu.VMEM((128, d), F32)],
        ),
        compiler_params=pltpu.CompilerParams(vmem_limit_bytes=40 << 20),
        cost_estimate=pl.CostEstimate(
            flops=2 * 128 * toks * d, bytes_accessed=2 * toks * d, transcendentals=0
        ),
    )(place, starts, hidden, gain)


RING = (0, -1, 1, -2, 2, -3, 3, 4)


def embed_kernel(place, col_starts, counts, *refs):
    blocks, out, got, sums, sems = refs[:9], refs[9], refs[10], refs[11], refs[12]
    copies = []
    for k in range(7):
        copies.append(pltpu.make_async_copy(blocks[k], got.at[k], sems.at[k]))
    copies.append(pltpu.make_async_copy(blocks[7], got.at[7, pl.ds(0, HALF_ROWS)], sems.at[7]))
    copies.append(
        pltpu.make_async_copy(
            blocks[8], got.at[7, pl.ds(HALF_ROWS, 528 - HALF_ROWS)], sems.at[8]
        )
    )
    for copy in copies:
        copy.start()
    z = place[1]

    def first_of(k):
        far = jnp.zeros(k.shape, jnp.int32)
        for n, shift in enumerate(RING):
            far = jnp.where(k == n, shift, far)
        dev = lax.rem(z + far + 8, 8)
        begun = (col_starts[...] <= dev * 1024).astype(jnp.int32)
        return jnp.sum(begun, axis=0, keepdims=True) - 1

    seg = lax.broadcasted_iota(jnp.int32, (256, 512), 0)
    lane = lax.broadcasted_iota(jnp.int32, (1, 512), 1)
    pick = (seg == first_of(lane // 64) + lane % 64).astype(F32).astype(BF)
    tlane = lax.broadcasted_iota(jnp.int32, (1, 128), 1)
    tail_hit = lax.broadcasted_iota(jnp.int32, (256, 128), 0) == first_of(tlane // 16) + 64
    for copy in copies:
        copy.wait()
    tail = jnp.concatenate([got[k, 512:528, :] for k in range(8)], axis=0)
    square = jnp.zeros((256, 1), F32)
    for g in range(8):
        main = jnp.concatenate([got[k, 64 * g : 64 * g + 64, :] for k in range(8)], axis=0)
        tpick = (tail_hit & (tlane % 16 == g)).astype(F32).astype(BF)
        mean = (
            jnp.dot(pick, main, preferred_element_type=F32)
            + jnp.dot(tpick, tail, preferred_element_type=F32)
        ) / counts[...]
        sums[:, 512 * g : 512 * g + 512] = mean
        square += jnp.sum(mean * mean, axis=1, keepdims=True)
    scale = lax.rsqrt(square + 1e-06)
    for g in range(8):
        cols = slice(512 * g, 512 * g + 512)
        out[:, cols] = (sums[:, cols] * scale).astype(BF)


def embed(place, col_starts, counts, blocks):
    any_spec = pl.BlockSpec(memory_space=pl.ANY)
    vmem = pl.BlockSpec(memory_space=pltpu.VMEM)
    return pl.pallas_call(
        embed_kernel,
        out_shape=jax.ShapeDtypeStruct((256, 4096), BF),
        in_specs=[pl.BlockSpec(memory_space=pltpu.SMEM), vmem, vmem] + [any_spec] * 9,
        out_specs=vmem,
        scratch_shapes=[
            pltpu.VMEM((8, 528, 512), BF),
            pltpu.VMEM((256, 4096), F32),
            pltpu.SemaphoreType.DMA((9,)),
        ],
        compiler_params=pltpu.CompilerParams(vmem_limit_bytes=40 << 20),
        cost_estimate=pl.CostEstimate(
            flops=2 * 256 * 640 * 4096, bytes_accessed=7 << 20, transcendentals=0
        ),
    )(place, col_starts, counts, *blocks)


def score_kernel(place, scale, ids, positive, mine, other, *refs):
    q_refs, out, wide_q, stats, sems = refs[:10], refs[10], refs[11], refs[12], refs[13]
    x, y = place[2], place[3]

    def block_of(n):
        return (0, -1, 1, 2)[n]

    copies = []

    def add(src, row, rows, dx, dy):
        chip = lax.rem(x + dx + 4, 4) * 4 + lax.rem(y + dy + 4, 4)
        cols = pl.ds(pl.multiple_of(chip * 256, 256), 256)
        copies.append(
            pltpu.make_async_copy(src, wide_q.at[pl.ds(row, rows), cols], sems.at[len(copies)])
        )

    for half in range(2):
        own, plus, minus, far_lo, far_hi = q_refs[5 * half : 5 * half + 5]
        base = 512 * half
        for n in range(4):
            near = block_of(n)
            for ref, row, rows, along in (
                (own, 0, 512, 0),
                (plus, 0, 512, -1),
                (minus, 0, 512, 1),
                (far_lo, 0, 256, 2),
                (far_hi, 256, 256, 2),
            ):
                dx, dy = (near, along) if half == 0 else (along, near)
                add(ref.at[n], base + row, rows, dx, dy)
    for copy in copies:
        copy.start()
    for copy in copies:
        copy.wait()
    tile = 256

    def body(t, carry):
        rows = pl.ds(pl.multiple_of(t * tile, tile), tile)
        q = wide_q[rows, :]
        wq = q.astype(F32)
        factor = scale[0] * lax.rsqrt(jnp.sum(wq * wq, axis=1, keepdims=True) + 1e-06)
        nt = (((1,), (1,)), ((), ()))
        s0 = lax.dot_general(q, mine[...], nt, preferred_element_type=F32) * factor
        s1 = lax.dot_general(q, other[...], nt, preferred_element_type=F32) * factor
        pos = positive[rows, :]
        chosen = jnp.sum(
            jnp.where(ids[:, 0:256] == pos, s0, 0.0) + jnp.where(ids[:, 256:512] == pos, s1, 0.0),
            axis=1,
            keepdims=True,
        )
        top = jnp.max(jnp.maximum(s0, s1), axis=1, keepdims=True)
        total = jnp.sum(jnp.exp(s0 - top) + jnp.exp(s1 - top), axis=1, keepdims=True)
        lane = lax.broadcasted_iota(jnp.int32, (tile, 128), 1)
        stats[rows, :] = jnp.where(
            lane == 0, top, jnp.where(lane == 1, total, jnp.where(lane == 2, chosen, 0.0))
        )
        return carry

    lax.fori_loop(0, 1024 // tile, body, 0)
    out[...] = jnp.transpose(stats[...])[0:8, :]


def score(place, scale, ids, positive, mine, other, blocks):
    any_spec = pl.BlockSpec(memory_space=pl.ANY)
    vmem = pl.BlockSpec(memory_space=pltpu.VMEM)
    smem = pl.BlockSpec(memory_space=pltpu.SMEM)
    return pl.pallas_call(
        score_kernel,
        out_shape=jax.ShapeDtypeStruct((8, 1024), F32),
        in_specs=[smem, smem, vmem, vmem, vmem, vmem] + [any_spec] * 10,
        out_specs=vmem,
        scratch_shapes=[
            pltpu.VMEM((1024, 4096), BF),
            pltpu.VMEM((1024, 128), F32),
            pltpu.SemaphoreType.DMA((40,)),
        ],
        compiler_params=pltpu.CompilerParams(vmem_limit_bytes=48 << 20),
        cost_estimate=pl.CostEstimate(
            flops=2 * 1024 * 512 * 4096, bytes_accessed=12 << 20, transcendentals=1024 * 512
        ),
    )(place, scale, ids, positive, mine, other, *blocks)


def merge(parts):
    top = parts[0][0]
    for p in parts[1:]:
        top = jnp.maximum(top, p[0])
    total = sum(p[1] * jnp.exp(p[0] - top) for p in parts)
    chosen = sum(p[2] for p in parts)
    return jnp.stack([top, total, chosen])


def per_device(hidden, gain, seg_start, owner, queries, positive, logit_scale):
    seq_count = lax.axis_size("seq")
    tok_count = hidden.shape[1]
    seg_count = seg_start.shape[1]
    seg_owned = seg_count // seq_count
    dp, z = lax.axis_index("dp"), lax.axis_index("seq")
    core = dp % NC
    place = jnp.stack([z * tok_count, z, dp // (NY * NC), (dp // NC) % NY]).astype(jnp.int32)
    quarter = queries.shape[0] // 4
    half = queries.shape[0] // 2

    own = lax.dynamic_slice_in_dim(queries, core * half, half)
    away = lax.dynamic_slice_in_dim(queries, (1 - core) * half, half)
    back = move(away, dc=1)
    block = jnp.where(
        core == 0, jnp.concatenate([own, back], 1), jnp.concatenate([back, own], 1)
    )
    a, b = block[:quarter], block[quarter:]
    a, b, hidden = barrier((a, b, hidden))
    a_near = (a, move(a, dx=1), move(a, dx=-1), move(a, dx=2))
    b_near = (b, move(b, dy=1), move(b, dy=-1), move(b, dy=2))

    packed = pool(place, seg_start, hidden[0], gain[None, :])
    ring = [packed, turn(packed, 1), turn(packed, -1)]

    a_line, b_line = jnp.stack(a_near), jnp.stack(b_near)
    a_line, b_line = barrier((a_line, b_line))
    a_plus, a_minus = move(a_line, dy=1), move(a_line, dy=-1)
    b_plus, b_minus = move(b_line, dx=1), move(b_line, dx=-1)
    for _ in range(2):
        ring[-2:] = barrier(tuple(ring[-2:]))
        ring += [turn(ring[-2], 1), turn(ring[-1], -1)]
    ring[-2:] = barrier(tuple(ring[-2:]))
    ring += [turn(ring[-2][:HALF_ROWS], 1), turn(ring[-1][HALF_ROWS:], -1)]
    eighth = quarter // 2
    a_plus, a_minus, b_plus, b_minus = barrier((a_plus, a_minus, b_plus, b_minus))
    a_far = (move(a_plus[:, :eighth], dy=1), move(a_minus[:, eighth:], dy=-1))
    b_far = (move(b_plus[:, :eighth], dx=1), move(b_minus[:, eighth:], dx=-1))

    starts = seg_start[0]
    ends = jnp.concatenate([starts[1:], jnp.full((1,), tok_count * seq_count, jnp.int32)])
    counts = (ends - starts).astype(F32)
    mine = embed(place, starts[:, None], counts[:, None], ring)
    other = move(mine, dc=1)

    seg = jnp.arange(seg_count, dtype=jnp.int32)
    ids = jnp.concatenate([dp * seg_count + seg, (dp + 1 - 2 * core) * seg_count + seg])[None, :]
    picks = lax.dynamic_slice_in_dim(positive, core * half, half)[:, None]
    blocks = [a_line, a_plus, a_minus, *a_far, b_line, b_plus, b_minus, *b_far]
    stats = score(place, logit_scale, ids, picks, mine, other, blocks)

    hold = owner[0] == z
    rank = jnp.cumsum(hold.astype(jnp.int32)) - 1
    pick = (
        hold[None, :] & (rank[None, :] == jnp.arange(seg_owned, dtype=jnp.int32)[:, None])
    ).astype(BF)
    pooled = jnp.dot(pick, mine, preferred_element_type=F32).astype(BF)

    stats = stats[:3]
    stats = merge([stats, move(stats, dx=1), move(stats, dx=-1), move(stats, dx=2)])
    stats = merge([stats, move(stats, dy=1), move(stats, dy=-1), move(stats, dy=2)])
    part = stats[2] - stats[0] - jnp.log(stats[1])
    rest = move(part, dc=1)
    log_prob = jnp.where(core == 0, jnp.concatenate([part, rest]), jnp.concatenate([rest, part]))
    return pooled, log_prob


def solution(mesh):
    in_specs = (
        P("dp", "seq", None),
        P(),
        P("dp", None),
        P("dp", None),
        P("seq", "dp"),
        P("seq"),
        P(),
    )
    out_specs = (P(("dp", "seq"), None), P("seq"))
    return jax.shard_map(
        per_device, mesh=mesh, in_specs=in_specs, out_specs=out_specs, check_vma=False
    )
```

```python
import jax
import jax.numpy as jnp
from jax import lax
from jax.experimental import pallas as pl
from jax.experimental.pallas import tpu as pltpu
from jax.sharding import PartitionSpec as P

NX, NY, NC, NZ = 4, 4, 2, 8
PACKED = 528
CUT = 256
RING = (0, -1, 1, -2, 2, -3, 3, 4)
BF = jnp.bfloat16
F32 = jnp.float32
barrier = lax.optimization_barrier


def along(core):
    return 1 - 2 * core


def move(value, dx=0, dy=0, dc=0):
    pairs = []
    for x in range(NX):
        for y in range(NY):
            for c in range(NC):
                to = (((x + dx) % NX) * NY + (y + dy) % NY) * NC + (c + dc) % NC
                pairs.append(((x * NY + y) * NC + c, to))
    return lax.ppermute(value, "dp", pairs)


def _hop(axis_and_step):
    pairs = []
    for x in range(NX):
        for y in range(NY):
            for c in range(NC):
                for z in range(NZ):
                    axis, step = axis_and_step(c)
                    to = [x, y, z]
                    to[axis] = (to[axis] + step) % (NX, NY, NZ)[axis]
                    here = ((x * NY + y) * NC + c) * NZ + z
                    pairs.append((here, ((to[0] * NY + to[1]) * NC + c) * NZ + to[2]))
    return pairs


def turn(value, step):
    return lax.ppermute(value, "seq", [(i, (i + step) % NZ) for i in range(NZ)])


def pass_on(value, second, step):
    return lax.ppermute(value, ("dp", "seq"), _hop(lambda c: ((c + second) % 2, step)))


def place():
    dp, z = lax.axis_index("dp"), lax.axis_index("seq")
    return lax.div(dp, NY * NC), lax.rem(lax.div(dp, NC), NY), lax.rem(dp, NC), z


def column(row):
    n = row.shape[1]
    same = lax.broadcasted_iota(jnp.int32, (n, n), 0) == lax.broadcasted_iota(jnp.int32, (n, n), 1)
    return jnp.sum(jnp.where(same, row, 0), axis=1, keepdims=True)


POOL_ROWS = 256


def pool_kernel(starts, owner, gain, hidden, out, info, pick, token, buf, weights, sems):
    toks = hidden.shape[1]
    steps = toks // POOL_ROWS
    copies = [
        pltpu.make_async_copy(hidden.at[0, pl.ds(POOL_ROWS * n, POOL_ROWS)], buf.at[pl.ds(POOL_ROWS * n, POOL_ROWS)], sems.at[n])
        for n in range(steps)
    ]
    for copy in copies:
        copy.start()
    z = lax.axis_index("seq")
    first = z * hidden.shape[1]
    length = hidden.shape[1] * NZ
    segs = starts.shape[1]
    from_row = starts[...]
    lane = lax.broadcasted_iota(jnp.int32, (segs, segs), 1)
    line = lax.broadcasted_iota(jnp.int32, (segs, segs), 0)
    begin = jnp.sum(jnp.where(lane == line, from_row, 0), axis=1, keepdims=True)
    end = jnp.sum(jnp.where(lane == line + 1, from_row, 0), axis=1, keepdims=True)
    end = jnp.where(lax.broadcasted_iota(jnp.int32, (segs, 1), 0) == segs - 1, length, end)
    token[...] = jnp.zeros_like(token)
    info[:, 0:128] = jnp.broadcast_to(begin, (segs, 128)).astype(F32)
    info[:, 128:256] = jnp.broadcast_to(end - begin, (segs, 128)).astype(F32)
    hold = (owner[...] == z).astype(jnp.int32)
    hold_col = jnp.sum(jnp.where(lane == line, hold, 0), axis=1, keepdims=True)
    rank = jnp.sum(jnp.where(line < lane, hold_col, 0), axis=0, keepdims=True)
    slot = lax.broadcasted_iota(jnp.int32, (pick.shape[0], segs), 0)
    pick[...] = jnp.where((rank == slot) & (hold == 1), 1.0, 0.0).astype(BF)

    before = jnp.sum((from_row <= first).astype(jnp.int32), axis=1, keepdims=True)
    for n in range(steps):
        copies[n].wait()
        wide = buf[POOL_ROWS * n : POOL_ROWS * n + POOL_ROWS, :].astype(F32)
        rate = lax.rsqrt(jnp.mean(wide * wide, axis=1, keepdims=True) + 1e-05)
        high = rate.astype(BF).astype(F32)
        pos = first + n * POOL_ROWS + lax.broadcasted_iota(jnp.int32, (POOL_ROWS, 1), 0)
        rel = jnp.sum((from_row <= pos).astype(jnp.int32), axis=1, keepdims=True) - before
        at = lax.broadcasted_iota(jnp.int32, (POOL_ROWS, 128), 1)
        weight = jnp.where((rel == at) & (at < 64), high, 0.0)
        weight = jnp.where((rel + 64 == at), rate - high, weight)
        weights[:, POOL_ROWS * n : POOL_ROWS * n + POOL_ROWS] = jnp.transpose(weight).astype(BF)
    weight = weights[...]
    end_weight = jnp.where(rel[POOL_ROWS - 16 :] == 64, rate[POOL_ROWS - 16 :], 0.0)
    tail = []
    for g in range(8):
        cols = slice(512 * g, 512 * g + 512)
        part = jnp.dot(weight, buf[:, cols], preferred_element_type=F32)
        out[64 * g : 64 * g + 64, :] = ((part[0:64] + part[64:128]) * gain[:, cols]).astype(BF)
        end_rows = buf[toks - 16 : toks, cols].astype(F32)
        tail.append(jnp.sum(end_rows * end_weight, axis=0, keepdims=True) * gain[:, cols])
    tail.append(jnp.zeros((8, 512), F32))
    out[512:528, :] = jnp.concatenate(tail, axis=0).astype(BF)


def pool(starts, owner, gain, hidden):
    _, toks, d = hidden.shape
    segs = starts.shape[1]
    vmem = pl.BlockSpec(memory_space=pltpu.VMEM)
    return pl.pallas_call(
        pool_kernel,
        out_shape=(
            jax.ShapeDtypeStruct((PACKED, 512), BF),
            jax.ShapeDtypeStruct((segs, 256), F32),
            jax.ShapeDtypeStruct((segs // NZ, segs), BF),
            jax.ShapeDtypeStruct((8, 128), F32),
        ),
        in_specs=[vmem, vmem, vmem, pl.BlockSpec(memory_space=pltpu.HBM)],
        out_specs=(vmem,) * 4,
        scratch_shapes=[
            pltpu.VMEM((toks, d), BF),
            pltpu.VMEM((128, toks), BF),
            pltpu.SemaphoreType.DMA((toks // POOL_ROWS,)),
        ],
        compiler_params=pltpu.CompilerParams(vmem_limit_bytes=56 << 20),
        cost_estimate=pl.CostEstimate(
            flops=2 * 128 * toks * d, bytes_accessed=2 * toks * d, transcendentals=0
        ),
    )(starts, owner, gain, hidden)


def embed_kernel(info, _, *refs):
    blocks, out, sums = refs[:9], refs[9], refs[10]
    z = lax.axis_index("seq")
    starts = info[:, 0:1]
    counts = info[:, 128:129]

    def first_of(k):
        far = jnp.zeros(k.shape, jnp.int32)
        for n, shift in enumerate(RING):
            far = jnp.where(k == n, shift, far)
        dev = lax.rem(z + far + 8, 8) * 1024
        begun = (starts <= dev.astype(F32)).astype(F32)
        return (jnp.sum(begun, axis=0, keepdims=True) - 1.0).astype(jnp.int32)

    seg = lax.broadcasted_iota(jnp.int32, (256, 512), 0)
    lane = lax.broadcasted_iota(jnp.int32, (1, 512), 1)
    pick = jnp.where(seg == first_of(lane // 64) + lane % 64, 1.0, 0.0).astype(BF)
    tlane = lax.broadcasted_iota(jnp.int32, (1, 128), 1)
    tail_hit = lax.broadcasted_iota(jnp.int32, (256, 128), 0) == first_of(tlane // 16) + 64

    def rows_of(row, rows):
        parts = [block[row : row + rows, :] for block in blocks[:7]]
        if row < CUT:
            parts.append(blocks[7][row : row + rows, :])
        else:
            parts.append(blocks[8][row - CUT : row - CUT + rows, :])
        return jnp.concatenate(parts, axis=0)

    tail = rows_of(512, 16)
    square = jnp.zeros((256, 1), F32)
    for g in range(8):
        tpick = jnp.where(tail_hit & (tlane % 16 == g), 1.0, 0.0).astype(BF)
        mean = (
            jnp.dot(pick, rows_of(64 * g, 64), preferred_element_type=F32)
            + jnp.dot(tpick, tail, preferred_element_type=F32)
        ) / counts
        sums[g] = mean
        square += jnp.sum(mean * mean, axis=1, keepdims=True)
    scale = lax.rsqrt(square + 1e-06)
    for g in range(8):
        out[:, 512 * g : 512 * g + 512] = (sums[g] * scale).astype(BF)


def embed(info, token, blocks):
    vmem = pl.BlockSpec(memory_space=pltpu.VMEM)
    return pl.pallas_call(
        embed_kernel,
        out_shape=jax.ShapeDtypeStruct((256, 4096), BF),
        in_specs=[vmem] * 11,
        out_specs=vmem,
        scratch_shapes=[pltpu.VMEM((8, 256, 512), F32)],
        compiler_params=pltpu.CompilerParams(vmem_limit_bytes=24 << 20),
        cost_estimate=pl.CostEstimate(
            flops=2 * 256 * 640 * 4096, bytes_accessed=7 << 20, transcendentals=0
        ),
    )(info, token, *blocks)


NEAR = (0, -1, 1, 2)


def query_block(refs, row, n, m):
    if m < 3:
        return refs[m][1024 * n + row : 1024 * n + row + 256, :]
    at = 1024 * (n % 2) + row
    return refs[3 + n // 2][at : at + 256, :]


def order_features(passages, ordered):
    x, y, core, _ = place()
    for n, u in enumerate(NEAR):
        for m, v in enumerate(NEAR):
            dx, dy = u + core * (v - u), v + core * (u - v)
            chip = lax.rem(x + dx + 4, 4) * 4 + lax.rem(y + dy + 4, 4)
            cols = pl.ds(pl.multiple_of(chip * 256, 256), 256)
            to = 256 * (n * 4 + m)
            ordered[:, to : to + 256] = passages[:, cols]


def picks_of(positive, row):
    core = lax.rem(lax.axis_index("dp"), NC)
    at = core * 8 + row // 128
    return jnp.concatenate(
        [column(positive[pl.ds(at, 1), :]), column(positive[pl.ds(at + 1, 1), :])], axis=0
    )


def lanes(*values):
    lane = lax.broadcasted_iota(jnp.int32, (256, 128), 1)
    out = jnp.zeros((256, 128), F32)
    for n, value in enumerate(values):
        out = jnp.where(lane == n, value, out)
    return out


NT = (((1,), (1,)), ((), ()))


def own_kernel(scale, positive, passages, *refs):
    q_refs, all_q, stats, ordered = refs[:5], refs[5], refs[6], refs[7]
    order_features(passages, ordered)
    ids = lax.axis_index("dp") * 256 + lax.broadcasted_iota(jnp.int32, (1, 256), 1)
    for row in (0, 256, 512, 768):
        q = jnp.concatenate(
            [query_block(q_refs, row, n, m) for n in range(4) for m in range(4)], axis=1
        )
        rows = slice(row, row + 256)
        all_q[rows, :] = q
        wq = q.astype(F32)
        factor = scale[0] * lax.rsqrt(jnp.sum(wq * wq, axis=1, keepdims=True) + 1e-06)
        scores = lax.dot_general(q, ordered[...], NT, preferred_element_type=F32) * factor
        hit = ids == picks_of(positive, row)
        chosen = jnp.sum(jnp.where(hit, scores, 0.0), axis=1, keepdims=True)
        top = jnp.max(scores, axis=1, keepdims=True)
        total = jnp.sum(jnp.exp(scores - top), axis=1, keepdims=True)
        stats[rows, :] = lanes(top, total, chosen, factor)


def other_kernel(positive, passages, all_q, early, out, ordered, stats):
    order_features(passages, ordered)
    dp = lax.axis_index("dp")
    first = (dp + along(lax.rem(dp, NC))) * 256
    ids = first + lax.broadcasted_iota(jnp.int32, (1, 256), 1)

    for row in (0, 256, 512, 768):
        rows = pl.ds(row, 256)
        have = early[rows, :]
        factor = have[:, 3:4]
        scores = lax.dot_general(all_q[rows, :], ordered[...], NT, preferred_element_type=F32)
        scores = scores * factor
        hit = ids == picks_of(positive, row)
        chosen = jnp.sum(jnp.where(hit, scores, 0.0), axis=1, keepdims=True) + have[:, 2:3]
        top = jnp.maximum(jnp.max(scores, axis=1, keepdims=True), have[:, 0:1])
        total = jnp.sum(jnp.exp(scores - top), axis=1, keepdims=True)
        total = total + have[:, 1:2] * jnp.exp(have[:, 0:1] - top)
        stats[rows, :] = lanes(top, total, chosen)
    out[...] = jnp.transpose(stats[...])[0:8, :]


def score(scale, positive, mine, other, blocks):
    vmem = pl.BlockSpec(memory_space=pltpu.VMEM)
    smem = pl.BlockSpec(memory_space=pltpu.SMEM)
    params = pltpu.CompilerParams(vmem_limit_bytes=24 << 20)
    cost = pl.CostEstimate(
        flops=2 * 1024 * 256 * 4096, bytes_accessed=1 << 20, transcendentals=1024 * 256
    )
    all_q, early = pl.pallas_call(
        own_kernel,
        out_shape=(
            jax.ShapeDtypeStruct((1024, 4096), BF),
            jax.ShapeDtypeStruct((1024, 128), F32),
        ),
        in_specs=[smem] + [vmem] * 7,
        out_specs=(vmem, vmem),
        scratch_shapes=[pltpu.VMEM((256, 4096), BF)],
        compiler_params=params,
        cost_estimate=cost,
    )(scale, positive, mine, *blocks)
    return pl.pallas_call(
        other_kernel,
        out_shape=jax.ShapeDtypeStruct((8, 1024), F32),
        in_specs=[vmem] * 4,
        out_specs=vmem,
        scratch_shapes=[pltpu.VMEM((256, 4096), BF), pltpu.VMEM((1024, 128), F32)],
        compiler_params=params,
        cost_estimate=cost,
    )(positive, other, all_q, early)


ANY = pl.BlockSpec(memory_space=pl.ANY)


def fence(token):
    return pl.pallas_call(
        lambda token, out: None,
        out_shape=jax.ShapeDtypeStruct(token.shape, token.dtype),
        in_specs=[ANY],
        out_specs=ANY,
        input_output_aliases={0: 0},
        compiler_params=pltpu.CompilerParams(vmem_limit_bytes=1 << 20),
        cost_estimate=pl.CostEstimate(flops=20 * 10**9, bytes_accessed=8192, transcendentals=0),
    )(token)


def copied(rows_out, cuts, *arrays):
    def kernel(*refs):
        ins, outs, sems = refs[: len(arrays)], refs[len(arrays) : -1], refs[-1]
        copies = [
            pltpu.make_async_copy(
                ins[i].at[pl.ds(at, rows)], outs[o].at[pl.ds(to, rows)], sems.at[n]
            )
            for n, (i, at, rows, o, to) in enumerate(cuts)
        ]
        for copy in copies:
            copy.start()
        for copy in copies:
            copy.wait()

    return pl.pallas_call(
        kernel,
        out_shape=tuple(jax.ShapeDtypeStruct((rows, arrays[0].shape[1]), BF) for rows in rows_out),
        in_specs=[ANY] * len(arrays),
        out_specs=(ANY,) * len(rows_out),
        scratch_shapes=[pltpu.SemaphoreType.DMA((len(cuts),))],
        compiler_params=pltpu.CompilerParams(vmem_limit_bytes=1 << 20),
        cost_estimate=pl.CostEstimate(flops=10**6, bytes_accessed=1 << 20, transcendentals=0),
    )(*arrays)


def merge(parts):
    top = parts[0][0]
    for p in parts[1:]:
        top = jnp.maximum(top, p[0])
    total = sum(p[1] * jnp.exp(p[0] - top) for p in parts)
    chosen = sum(p[2] for p in parts)
    return jnp.stack([top, total, chosen])


def per_device(hidden, gain, seg_start, owner, queries, positive, logit_scale):
    core = lax.axis_index("dp") % NC
    half = queries.shape[0] // 2

    own = lax.dynamic_slice_in_dim(queries, core * half, half)
    away = lax.dynamic_slice_in_dim(queries, (1 - core) * half, half)
    back = move(away, dc=1)
    block = jnp.where(
        core == 0, jnp.concatenate([own, back], 1), jnp.concatenate([back, own], 1)
    )
    packed, info, pick, token = pool(seg_start, owner, gain[None, :], hidden)

    got = {("q", 0): block, ("f", 0): packed, ("b", 0): packed}
    last = []
    token = [token]

    def take(names):
        keys = [*names, *(k for k in last if k not in names)]
        *tied, mark = barrier((*(got[k] for k in keys), token[0]))
        got.update(zip(keys, tied))
        token[0] = fence(mark)
        last[:] = names

    def step(*names):
        take([(stream, n - 1) for stream, n in names])
        for stream, n in names:
            got[stream, n] = turn(got[stream, n - 1], 1 if stream == "f" else -1)

    got["f", 1], got["b", 1] = turn(packed, 1), turn(packed, -1)
    take([("q", 0)])
    got["+", 1], got["-", 1] = pass_on(got["q", 0], 0, 1), pass_on(got["q", 0], 0, -1)
    got["far", 1] = pass_on(got["q", 0], 0, 2)
    step(("f", 2), ("b", 2))
    take([("+", 1), ("-", 1), ("far", 1)])
    cuts = [(n, 0, half, 0, half * n) for n in range(4)]
    (line,) = copied((4 * half,), cuts, block, got["+", 1], got["-", 1], got["far", 1])
    got["+", 3], got["-", 3] = pass_on(line, 1, 1), pass_on(line, 1, -1)
    step(("f", 3), ("b", 3))
    take([("+", 3), ("-", 3)])
    cuts = [(0, 0, 2 * half, 0, 0), (1, 2 * half, 2 * half, 1, 0)]
    up, down = copied((2 * half, 2 * half), cuts, got["+", 3], got["-", 3])
    got["+", 4], got["-", 4] = pass_on(up, 1, 1), pass_on(down, 1, -1)
    take([("f", 3), ("b", 3)])
    cuts = [(0, 0, CUT, 0, 0), (1, CUT, PACKED - CUT, 1, 0)]
    up, down = copied((CUT, PACKED - CUT), cuts, got["f", 3], got["b", 3])
    got["f", 4], got["b", 4] = turn(up, 1), turn(down, -1)

    order = [packed, *(got[k, n] for n in (1, 2, 3, 4) for k in "fb")]
    mine = embed(info, token[0], order)
    late = [("+", 4), ("-", 4)]
    mine, *rest = barrier((mine, *(got[k] for k in late)))
    got.update(zip(late, rest))
    other = move(mine, dc=1)
    blocks = [line, *(got[k] for k in (("+", 3), ("-", 3), ("+", 4), ("-", 4)))]
    stats = score(logit_scale, positive.reshape(16, 128), mine, other, blocks)
    pooled = jnp.dot(pick, mine, preferred_element_type=F32).astype(BF)

    stats = stats[:3]
    stats = merge([stats, move(stats, dx=1), move(stats, dx=-1), move(stats, dx=2)])
    stats = merge([stats, move(stats, dy=1), move(stats, dy=-1), move(stats, dy=2)])
    part = stats[2] - stats[0] - jnp.log(stats[1])
    rest = move(part, dc=1)
    log_prob = jnp.where(core == 0, jnp.concatenate([part, rest]), jnp.concatenate([rest, part]))
    return pooled, log_prob


def solution(mesh):
    in_specs = (
        P("dp", "seq", None),
        P(),
        P("dp", None),
        P("dp", None),
        P("seq", "dp"),
        P("seq"),
        P(),
    )
    out_specs = (P(("dp", "seq"), None), P("seq"))
    return jax.shard_map(
        per_device, mesh=mesh, in_specs=in_specs, out_specs=out_specs, check_vma=False
    )
```

```python
import jax
import jax.numpy as jnp
from jax import lax
from jax.experimental import pallas as pl
from jax.experimental.pallas import tpu as pltpu
from jax.sharding import PartitionSpec as P

NX, NY, NC, NZ = 4, 4, 2, 8
PACKED = 528
CUT = 256
RING = (0, -1, 1, -2, 2, -3, 3, 4)
BF = jnp.bfloat16
F32 = jnp.float32
barrier = lax.optimization_barrier


def along(core):
    return 1 - 2 * core


def move(value, dx=0, dy=0, dc=0):
    pairs = []
    for x in range(NX):
        for y in range(NY):
            for c in range(NC):
                to = (((x + dx) % NX) * NY + (y + dy) % NY) * NC + (c + dc) % NC
                pairs.append(((x * NY + y) * NC + c, to))
    return lax.ppermute(value, "dp", pairs)


def _hop(axis_and_step):
    pairs = []
    for x in range(NX):
        for y in range(NY):
            for c in range(NC):
                for z in range(NZ):
                    axis, step = axis_and_step(c)
                    to = [x, y, z]
                    to[axis] = (to[axis] + step) % (NX, NY, NZ)[axis]
                    here = ((x * NY + y) * NC + c) * NZ + z
                    pairs.append((here, ((to[0] * NY + to[1]) * NC + c) * NZ + to[2]))
    return pairs


def turn(value, step):
    return lax.ppermute(value, ("dp", "seq"), _hop(lambda c: (2, step * along(c))))


def pass_on(value, second, step):
    return lax.ppermute(value, ("dp", "seq"), _hop(lambda c: ((c + second) % 2, step)))


def place():
    dp, z = lax.axis_index("dp"), lax.axis_index("seq")
    return lax.div(dp, NY * NC), lax.rem(lax.div(dp, NC), NY), lax.rem(dp, NC), z


def column(row):
    n = row.shape[1]
    same = lax.broadcasted_iota(jnp.int32, (n, n), 0) == lax.broadcasted_iota(jnp.int32, (n, n), 1)
    return jnp.sum(jnp.where(same, row, 0), axis=1, keepdims=True)


POOL_ROWS = 256


def pool_kernel(starts, hidden, out, info, token, buf, weights, sems):
    toks = hidden.shape[1]
    steps = toks // POOL_ROWS
    copies = [
        pltpu.make_async_copy(hidden.at[0, pl.ds(POOL_ROWS * n, POOL_ROWS)], buf.at[pl.ds(POOL_ROWS * n, POOL_ROWS)], sems.at[n])
        for n in range(steps)
    ]
    for copy in copies:
        copy.start()
    z = lax.axis_index("seq")
    first = z * hidden.shape[1]
    length = hidden.shape[1] * NZ
    segs = starts.shape[1]
    from_row = starts[...]
    lane = lax.broadcasted_iota(jnp.int32, (segs, segs), 1)
    line = lax.broadcasted_iota(jnp.int32, (segs, segs), 0)
    begin = jnp.sum(jnp.where(lane == line, from_row, 0), axis=1, keepdims=True)
    end = jnp.sum(jnp.where(lane == line + 1, from_row, 0), axis=1, keepdims=True)
    end = jnp.where(lax.broadcasted_iota(jnp.int32, (segs, 1), 0) == segs - 1, length, end)
    token[...] = jnp.zeros_like(token)
    info[:, 0:128] = jnp.broadcast_to(begin, (segs, 128)).astype(F32)
    info[:, 128:256] = jnp.broadcast_to(end - begin, (segs, 128)).astype(F32)

    before = jnp.sum((from_row <= first).astype(jnp.int32), axis=1, keepdims=True)
    for n in range(steps):
        copies[n].wait()
        wide = buf[POOL_ROWS * n : POOL_ROWS * n + POOL_ROWS, :].astype(F32)
        rate = lax.rsqrt(jnp.mean(wide * wide, axis=1, keepdims=True) + 1e-05)
        high = rate.astype(BF).astype(F32)
        pos = first + n * POOL_ROWS + lax.broadcasted_iota(jnp.int32, (POOL_ROWS, 1), 0)
        rel = jnp.sum((from_row <= pos).astype(jnp.int32), axis=1, keepdims=True) - before
        at = lax.broadcasted_iota(jnp.int32, (POOL_ROWS, 128), 1)
        weight = jnp.where((rel == at) & (at < 64), high, 0.0)
        weight = jnp.where((rel + 64 == at), rate - high, weight)
        weights[:, POOL_ROWS * n : POOL_ROWS * n + POOL_ROWS] = jnp.transpose(weight).astype(BF)
    weight = weights[...]
    end_weight = jnp.where(rel[POOL_ROWS - 16 :] == 64, rate[POOL_ROWS - 16 :], 0.0)
    tail = []
    for g in range(8):
        cols = slice(512 * g, 512 * g + 512)
        part = jnp.dot(weight, buf[:, cols], preferred_element_type=F32)
        out[64 * g : 64 * g + 64, :] = (part[0:64] + part[64:128]).astype(BF)
        end_rows = buf[toks - 16 : toks, cols].astype(F32)
        tail.append(jnp.sum(end_rows * end_weight, axis=0, keepdims=True))
    tail.append(jnp.zeros((8, 512), F32))
    out[512:528, :] = jnp.concatenate(tail, axis=0).astype(BF)


def pool(starts, hidden):
    _, toks, d = hidden.shape
    segs = starts.shape[1]
    vmem = pl.BlockSpec(memory_space=pltpu.VMEM)
    return pl.pallas_call(
        pool_kernel,
        out_shape=(
            jax.ShapeDtypeStruct((PACKED, 512), BF),
            jax.ShapeDtypeStruct((segs, 256), F32),
            jax.ShapeDtypeStruct((8, 128), F32),
        ),
        in_specs=[vmem, pl.BlockSpec(memory_space=pltpu.HBM)],
        out_specs=(vmem,) * 3,
        scratch_shapes=[
            pltpu.VMEM((toks, d), BF),
            pltpu.VMEM((128, toks), BF),
            pltpu.SemaphoreType.DMA((toks // POOL_ROWS,)),
        ],
        compiler_params=pltpu.CompilerParams(vmem_limit_bytes=50 << 20),
        cost_estimate=pl.CostEstimate(
            flops=2 * 128 * toks * d, bytes_accessed=2 * toks * d, transcendentals=0
        ),
    )(starts, hidden)


def embed_kernel(info, _, gain, *refs):
    blocks, out, sums = refs[:9], refs[9], refs[10]
    _, _, core, z = place()
    way = along(core)
    starts = info[:, 0:1]
    counts = info[:, 128:129]

    def first_of(k):
        far = jnp.zeros(k.shape, jnp.int32)
        for n, shift in enumerate(RING):
            far = jnp.where(k == n, shift, far)
        dev = lax.rem(z + way * far + 8, 8) * 1024
        begun = (starts <= dev.astype(F32)).astype(F32)
        return (jnp.sum(begun, axis=0, keepdims=True) - 1.0).astype(jnp.int32)

    seg = lax.broadcasted_iota(jnp.int32, (256, 512), 0)
    lane = lax.broadcasted_iota(jnp.int32, (1, 512), 1)
    pick = jnp.where(seg == first_of(lane // 64) + lane % 64, 1.0, 0.0).astype(BF)
    tlane = lax.broadcasted_iota(jnp.int32, (1, 128), 1)
    tail_hit = lax.broadcasted_iota(jnp.int32, (256, 128), 0) == first_of(tlane // 16) + 64

    def rows_of(row, rows):
        parts = [block[row : row + rows, :] for block in blocks[:7]]
        if row < CUT:
            parts.append(blocks[7][row : row + rows, :])
        else:
            parts.append(blocks[8][row - CUT : row - CUT + rows, :])
        return jnp.concatenate(parts, axis=0)

    tail = rows_of(512, 16)
    square = jnp.zeros((256, 1), F32)
    for g in range(8):
        tpick = jnp.where(tail_hit & (tlane % 16 == g), 1.0, 0.0).astype(BF)
        mean = (
            jnp.dot(pick, rows_of(64 * g, 64), preferred_element_type=F32)
            + jnp.dot(tpick, tail, preferred_element_type=F32)
        ) * gain[:, 512 * g : 512 * g + 512] / counts
        sums[g] = mean
        square += jnp.sum(mean * mean, axis=1, keepdims=True)
    scale = lax.rsqrt(square + 1e-06)
    for g in range(8):
        out[:, 512 * g : 512 * g + 512] = (sums[g] * scale).astype(BF)


def embed(info, token, gain, blocks):
    vmem = pl.BlockSpec(memory_space=pltpu.VMEM)
    return pl.pallas_call(
        embed_kernel,
        out_shape=jax.ShapeDtypeStruct((256, 4096), BF),
        in_specs=[vmem] * 12,
        out_specs=vmem,
        scratch_shapes=[pltpu.VMEM((8, 256, 512), F32)],
        compiler_params=pltpu.CompilerParams(vmem_limit_bytes=24 << 20),
        cost_estimate=pl.CostEstimate(
            flops=2 * 256 * 640 * 4096, bytes_accessed=7 << 20, transcendentals=0
        ),
    )(info, token, gain, *blocks)


def owned_kernel(owner, passages, out):
    hold = (owner[...] == lax.axis_index("seq")).astype(jnp.int32)
    segs = owner.shape[1]
    line = lax.broadcasted_iota(jnp.int32, (segs, segs), 0)
    lane = lax.broadcasted_iota(jnp.int32, (segs, segs), 1)
    rank = jnp.sum(jnp.where(line < lane, column(hold), 0), axis=0, keepdims=True)
    slot = lax.broadcasted_iota(jnp.int32, (out.shape[0], segs), 0)
    pick = jnp.where((rank == slot) & (hold == 1), 1.0, 0.0).astype(BF)
    out[...] = jnp.dot(pick, passages[...], preferred_element_type=F32).astype(BF)


def owned(owner, passages):
    vmem = pl.BlockSpec(memory_space=pltpu.VMEM)
    return pl.pallas_call(
        owned_kernel,
        out_shape=jax.ShapeDtypeStruct((passages.shape[0] // NZ, passages.shape[1]), BF),
        in_specs=[vmem] * 2,
        out_specs=vmem,
        compiler_params=pltpu.CompilerParams(vmem_limit_bytes=16 << 20),
        cost_estimate=pl.CostEstimate(
            flops=2 * 32 * 256 * 4096, bytes_accessed=3 << 20, transcendentals=0
        ),
    )(owner, passages)


NEAR = (0, -1, 1, 2)


def query_block(refs, row, n, m):
    if m < 3:
        return refs[m][1024 * n + row : 1024 * n + row + 256, :]
    at = 1024 * (n % 2) + row
    return refs[3 + n // 2][at : at + 256, :]


def order_features(passages, ordered):
    x, y, core, _ = place()
    for n, u in enumerate(NEAR):
        for m, v in enumerate(NEAR):
            dx, dy = u + core * (v - u), v + core * (u - v)
            chip = lax.rem(x + dx + 4, 4) * 4 + lax.rem(y + dy + 4, 4)
            cols = pl.ds(pl.multiple_of(chip * 256, 256), 256)
            to = 256 * (n * 4 + m)
            ordered[:, to : to + 256] = passages[:, cols]


def picks_of(positive, row):
    core = lax.rem(lax.axis_index("dp"), NC)
    at = core * 8 + row // 128
    return jnp.concatenate(
        [column(positive[pl.ds(at, 1), :]), column(positive[pl.ds(at + 1, 1), :])], axis=0
    )


def lanes(*values):
    lane = lax.broadcasted_iota(jnp.int32, (256, 128), 1)
    out = jnp.zeros((256, 128), F32)
    for n, value in enumerate(values):
        out = jnp.where(lane == n, value, out)
    return out


NT = (((1,), (1,)), ((), ()))


def own_kernel(scale, positive, passages, *refs):
    q_refs, all_q, stats, ordered = refs[:5], refs[5], refs[6], refs[7]
    order_features(passages, ordered)
    ids = lax.axis_index("dp") * 256 + lax.broadcasted_iota(jnp.int32, (1, 256), 1)
    for row in (0, 256, 512, 768):
        q = jnp.concatenate(
            [query_block(q_refs, row, n, m) for n in range(4) for m in range(4)], axis=1
        )
        rows = slice(row, row + 256)
        all_q[rows, :] = q
        wq = q.astype(F32)
        factor = scale[...] * lax.rsqrt(jnp.sum(wq * wq, axis=1, keepdims=True) + 1e-06)
        scores = lax.dot_general(q, ordered[...], NT, preferred_element_type=F32) * factor
        hit = ids == picks_of(positive, row)
        chosen = jnp.sum(jnp.where(hit, scores, 0.0), axis=1, keepdims=True)
        top = jnp.max(scores, axis=1, keepdims=True)
        total = jnp.sum(jnp.exp(scores - top), axis=1, keepdims=True)
        stats[rows, :] = lanes(top, total, chosen, factor)


def other_kernel(positive, passages, all_q, early, out, ordered, stats):
    order_features(passages, ordered)
    dp = lax.axis_index("dp")
    first = (dp + along(lax.rem(dp, NC))) * 256
    ids = first + lax.broadcasted_iota(jnp.int32, (1, 256), 1)

    for row in (0, 256, 512, 768):
        rows = pl.ds(row, 256)
        have = early[rows, :]
        factor = have[:, 3:4]
        scores = lax.dot_general(all_q[rows, :], ordered[...], NT, preferred_element_type=F32)
        scores = scores * factor
        hit = ids == picks_of(positive, row)
        chosen = jnp.sum(jnp.where(hit, scores, 0.0), axis=1, keepdims=True) + have[:, 2:3]
        top = jnp.maximum(jnp.max(scores, axis=1, keepdims=True), have[:, 0:1])
        total = jnp.sum(jnp.exp(scores - top), axis=1, keepdims=True)
        total = total + have[:, 1:2] * jnp.exp(have[:, 0:1] - top)
        stats[rows, :] = lanes(top, total, chosen)
    out[...] = jnp.transpose(stats[...])[0:8, :]


def score(scale, positive, mine, other, blocks):
    vmem = pl.BlockSpec(memory_space=pltpu.VMEM)
    params = pltpu.CompilerParams(vmem_limit_bytes=24 << 20)
    cost = pl.CostEstimate(
        flops=2 * 1024 * 256 * 4096, bytes_accessed=1 << 20, transcendentals=1024 * 256
    )
    all_q, early = pl.pallas_call(
        own_kernel,
        out_shape=(
            jax.ShapeDtypeStruct((1024, 4096), BF),
            jax.ShapeDtypeStruct((1024, 128), F32),
        ),
        in_specs=[vmem] * 8,
        out_specs=(vmem, vmem),
        scratch_shapes=[pltpu.VMEM((256, 4096), BF)],
        compiler_params=params,
        cost_estimate=cost,
    )(scale.reshape(1, 1), positive, mine, *blocks)
    return pl.pallas_call(
        other_kernel,
        out_shape=jax.ShapeDtypeStruct((8, 1024), F32),
        in_specs=[vmem] * 4,
        out_specs=vmem,
        scratch_shapes=[pltpu.VMEM((256, 4096), BF), pltpu.VMEM((1024, 128), F32)],
        compiler_params=params,
        cost_estimate=cost,
    )(positive, other, all_q, early)


ANY = pl.BlockSpec(memory_space=pl.ANY)


def fence(token):
    return pl.pallas_call(
        lambda token, out: None,
        out_shape=jax.ShapeDtypeStruct(token.shape, token.dtype),
        in_specs=[ANY],
        out_specs=ANY,
        input_output_aliases={0: 0},
        compiler_params=pltpu.CompilerParams(vmem_limit_bytes=1 << 20),
        cost_estimate=pl.CostEstimate(flops=20 * 10**9, bytes_accessed=8192, transcendentals=0),
    )(token)


def copied(rows_out, cuts, *arrays):
    def kernel(*refs):
        ins, outs, sems = refs[: len(arrays)], refs[len(arrays) : -1], refs[-1]
        copies = [
            pltpu.make_async_copy(
                ins[i].at[pl.ds(at, rows)], outs[o].at[pl.ds(to, rows)], sems.at[n]
            )
            for n, (i, at, rows, o, to) in enumerate(cuts)
        ]
        for copy in copies:
            copy.start()
        for copy in copies:
            copy.wait()

    return pl.pallas_call(
        kernel,
        out_shape=tuple(jax.ShapeDtypeStruct((rows, arrays[0].shape[1]), BF) for rows in rows_out),
        in_specs=[ANY] * len(arrays),
        out_specs=(ANY,) * len(rows_out),
        scratch_shapes=[pltpu.SemaphoreType.DMA((len(cuts),))],
        compiler_params=pltpu.CompilerParams(vmem_limit_bytes=1 << 20),
        cost_estimate=pl.CostEstimate(flops=10**6, bytes_accessed=1 << 20, transcendentals=0),
    )(*arrays)


def merge(parts):
    top = parts[0][0]
    for p in parts[1:]:
        top = jnp.maximum(top, p[0])
    total = sum(p[1] * jnp.exp(p[0] - top) for p in parts)
    chosen = sum(p[2] for p in parts)
    return jnp.stack([top, total, chosen])


def per_device(hidden, gain, seg_start, owner, queries, positive, logit_scale):
    core = lax.axis_index("dp") % NC
    half = queries.shape[0] // 2

    own = lax.dynamic_slice_in_dim(queries, core * half, half)
    away = lax.dynamic_slice_in_dim(queries, (1 - core) * half, half)
    back = move(away, dc=1)
    block = jnp.where(
        core == 0, jnp.concatenate([own, back], 1), jnp.concatenate([back, own], 1)
    )
    packed, info, token = pool(seg_start, hidden)

    got = {("q", 0): block, ("f", 0): packed, ("b", 0): packed}
    last = []
    token = [token]

    def take(names, hold=False):
        keys = [*names, *(k for k in last if k not in names)]
        *tied, mark = barrier((*(got[k] for k in keys), token[0]))
        got.update(zip(keys, tied))
        token[0] = fence(mark) if hold else mark
        last[:] = names

    def step(*names):
        take([(stream, n - 1) for stream, n in names], hold=True)
        for stream, n in names:
            got[stream, n] = turn(got[stream, n - 1], 1 if stream == "f" else -1)

    take([("q", 0)], hold=True)
    got["+", 1], got["-", 1] = pass_on(got["q", 0], 0, 1), pass_on(got["q", 0], 0, -1)
    got["far", 1] = pass_on(got["q", 0], 0, 2)
    step(("f", 1), ("b", 1))
    take([("+", 1), ("-", 1), ("far", 1)], hold=True)
    cuts = [(n, 0, half, 0, half * n) for n in range(4)]
    (line,) = copied((4 * half,), cuts, block, got["+", 1], got["-", 1], got["far", 1])
    got["+", 3], got["-", 3] = pass_on(line, 1, 1), pass_on(line, 1, -1)
    step(("f", 2), ("b", 2))
    step(("f", 3), ("b", 3))
    take([("+", 3), ("-", 3)], hold=True)
    cuts = [(0, 0, 2 * half, 0, 0), (1, 2 * half, 2 * half, 1, 0)]
    up, down = copied((2 * half, 2 * half), cuts, got["+", 3], got["-", 3])
    got["+", 4], got["-", 4] = pass_on(up, 1, 1), pass_on(down, 1, -1)
    take([("f", 3), ("b", 3)])
    cuts = [(0, 0, CUT, 0, 0), (1, CUT, PACKED - CUT, 1, 0)]
    up, down = copied((CUT, PACKED - CUT), cuts, got["f", 3], got["b", 3])
    got["f", 4], got["b", 4] = turn(up, 1), turn(down, -1)

    order = [packed, *(got[k, n] for n in (1, 2, 3, 4) for k in "fb")]
    mine = embed(info, token[0], gain[None, :], order)
    late = [("+", 4), ("-", 4)]
    mine, *rest = barrier((mine, *(got[k] for k in late)))
    got.update(zip(late, rest))
    other = move(mine, dc=1)
    blocks = [line, *(got[k] for k in (("+", 3), ("-", 3), ("+", 4), ("-", 4)))]
    stats = score(logit_scale, positive.reshape(16, 128), mine, other, blocks)
    pooled = owned(owner, mine)

    stats = stats[:3]
    stats = merge([stats, move(stats, dx=1), move(stats, dx=-1), move(stats, dx=2)])
    stats, pooled = barrier((stats, pooled))
    stats = merge([stats, move(stats, dy=1), move(stats, dy=-1), move(stats, dy=2)])
    part = stats[2] - stats[0] - jnp.log(stats[1])
    rest = move(part, dc=1)
    log_prob = jnp.where(core == 0, jnp.concatenate([part, rest]), jnp.concatenate([rest, part]))
    return pooled, log_prob


def solution(mesh):
    in_specs = (
        P("dp", "seq", None),
        P(),
        P("dp", None),
        P("dp", None),
        P("seq", "dp"),
        P("seq"),
        P(),
    )
    out_specs = (P(("dp", "seq"), None), P("seq"))
    return jax.shard_map(
        per_device, mesh=mesh, in_specs=in_specs, out_specs=out_specs, check_vma=False
    )
```

```python
import jax
import jax.numpy as jnp
from jax import lax
from jax.experimental import pallas as pl
from jax.experimental.pallas import tpu as pltpu
from jax.sharding import PartitionSpec as P

NX, NY, NC, NZ = 4, 4, 2, 8
PACKED = 528
CUT = 256
RING = (0, -1, 1, -2, 2, -3, 3, 4)
BF = jnp.bfloat16
F32 = jnp.float32
barrier = lax.optimization_barrier


def along(core):
    return 1 - 2 * core


def move(value, dx=0, dy=0, dc=0):
    pairs = []
    for x in range(NX):
        for y in range(NY):
            for c in range(NC):
                to = (((x + dx) % NX) * NY + (y + dy) % NY) * NC + (c + dc) % NC
                pairs.append(((x * NY + y) * NC + c, to))
    return lax.ppermute(value, "dp", pairs)


def _hop(axis_and_step):
    pairs = []
    for x in range(NX):
        for y in range(NY):
            for c in range(NC):
                for z in range(NZ):
                    axis, step = axis_and_step(c)
                    to = [x, y, z]
                    to[axis] = (to[axis] + step) % (NX, NY, NZ)[axis]
                    here = ((x * NY + y) * NC + c) * NZ + z
                    pairs.append((here, ((to[0] * NY + to[1]) * NC + c) * NZ + to[2]))
    return pairs


def turn(value, step):
    return lax.ppermute(value, ("dp", "seq"), _hop(lambda c: (2, step * along(c))))


def pass_on(value, second, step):
    return lax.ppermute(value, ("dp", "seq"), _hop(lambda c: ((c + second) % 2, step)))


def place():
    dp, z = lax.axis_index("dp"), lax.axis_index("seq")
    return lax.div(dp, NY * NC), lax.rem(lax.div(dp, NC), NY), lax.rem(dp, NC), z


def column(row):
    n = row.shape[1]
    same = lax.broadcasted_iota(jnp.int32, (n, n), 0) == lax.broadcasted_iota(jnp.int32, (n, n), 1)
    return jnp.sum(jnp.where(same, row, 0), axis=1, keepdims=True)


POOL_ROWS = 256


def pool_kernel(starts, hidden, out, info, token, buf, weights, sems):
    toks = hidden.shape[1]
    steps = toks // POOL_ROWS
    copies = [
        pltpu.make_async_copy(hidden.at[0, pl.ds(POOL_ROWS * n, POOL_ROWS)], buf.at[pl.ds(POOL_ROWS * n, POOL_ROWS)], sems.at[n])
        for n in range(steps)
    ]
    for copy in copies:
        copy.start()
    z = lax.axis_index("seq")
    first = z * hidden.shape[1]
    length = hidden.shape[1] * NZ
    segs = starts.shape[1]
    from_row = starts[...]
    lane = lax.broadcasted_iota(jnp.int32, (segs, segs), 1)
    line = lax.broadcasted_iota(jnp.int32, (segs, segs), 0)
    begin = jnp.sum(jnp.where(lane == line, from_row, 0), axis=1, keepdims=True)
    end = jnp.sum(jnp.where(lane == line + 1, from_row, 0), axis=1, keepdims=True)
    end = jnp.where(lax.broadcasted_iota(jnp.int32, (segs, 1), 0) == segs - 1, length, end)
    token[...] = jnp.zeros_like(token)
    info[:, 0:128] = jnp.broadcast_to(begin, (segs, 128)).astype(F32)
    info[:, 128:256] = jnp.broadcast_to(end - begin, (segs, 128)).astype(F32)

    before = jnp.sum((from_row <= first).astype(jnp.int32), axis=1, keepdims=True)
    for n in range(steps):
        copies[n].wait()
        wide = buf[POOL_ROWS * n : POOL_ROWS * n + POOL_ROWS, :].astype(F32)
        rate = lax.rsqrt(jnp.mean(wide * wide, axis=1, keepdims=True) + 1e-05)
        high = rate.astype(BF).astype(F32)
        pos = first + n * POOL_ROWS + lax.broadcasted_iota(jnp.int32, (POOL_ROWS, 1), 0)
        rel = jnp.sum((from_row <= pos).astype(jnp.int32), axis=1, keepdims=True) - before
        at = lax.broadcasted_iota(jnp.int32, (POOL_ROWS, 128), 1)
        weight = jnp.where((rel == at) & (at < 64), high, 0.0)
        weight = jnp.where((rel + 64 == at), rate - high, weight)
        weights[:, POOL_ROWS * n : POOL_ROWS * n + POOL_ROWS] = jnp.transpose(weight).astype(BF)
    weight = weights[...]
    end_weight = jnp.where(rel[POOL_ROWS - 16 :] == 64, rate[POOL_ROWS - 16 :], 0.0)
    tail = []
    for g in range(8):
        cols = slice(512 * g, 512 * g + 512)
        part = jnp.dot(weight, buf[:, cols], preferred_element_type=F32)
        out[64 * g : 64 * g + 64, :] = (part[0:64] + part[64:128]).astype(BF)
        end_rows = buf[toks - 16 : toks, cols].astype(F32)
        tail.append(jnp.sum(end_rows * end_weight, axis=0, keepdims=True))
    tail.append(jnp.zeros((8, 512), F32))
    out[512:528, :] = jnp.concatenate(tail, axis=0).astype(BF)


def pool(starts, hidden):
    _, toks, d = hidden.shape
    segs = starts.shape[1]
    vmem = pl.BlockSpec(memory_space=pltpu.VMEM)
    return pl.pallas_call(
        pool_kernel,
        out_shape=(
            jax.ShapeDtypeStruct((PACKED, 512), BF),
            jax.ShapeDtypeStruct((segs, 256), F32),
            jax.ShapeDtypeStruct((8, 128), F32),
        ),
        in_specs=[vmem, pl.BlockSpec(memory_space=pltpu.HBM)],
        out_specs=(vmem,) * 3,
        scratch_shapes=[
            pltpu.VMEM((toks, d), BF),
            pltpu.VMEM((128, toks), BF),
            pltpu.SemaphoreType.DMA((toks // POOL_ROWS,)),
        ],
        compiler_params=pltpu.CompilerParams(vmem_limit_bytes=50 << 20),
        cost_estimate=pl.CostEstimate(
            flops=2 * 128 * toks * d, bytes_accessed=2 * toks * d, transcendentals=0
        ),
    )(starts, hidden)


def picks_for(info, ring):
    _, _, core, z = place()
    starts = info[:, 0:1]
    count = len(ring)

    def first_of(k):
        far = jnp.zeros(k.shape, jnp.int32)
        for n, shift in enumerate(ring):
            far = jnp.where(k == n, shift, far)
        dev = lax.rem(z + along(core) * far + 8, 8) * 1024
        begun = (starts <= dev.astype(F32)).astype(F32)
        return (jnp.sum(begun, axis=0, keepdims=True) - 1.0).astype(jnp.int32)

    seg = lax.broadcasted_iota(jnp.int32, (256, 64 * count), 0)
    lane = lax.broadcasted_iota(jnp.int32, (1, 64 * count), 1)
    pick = jnp.where(seg == first_of(lane // 64) + lane % 64, 1.0, 0.0).astype(BF)
    tlane = lax.broadcasted_iota(jnp.int32, (1, 16 * count), 1)
    tseg = lax.broadcasted_iota(jnp.int32, (256, 16 * count), 0)
    tail_hit = tseg == first_of(tlane // 16) + 64
    return pick, lambda g: jnp.where(tail_hit & (tlane % 16 == g), 1.0, 0.0).astype(BF)


def gather_kernel(info, *refs):
    blocks, sums = refs[:7], refs[7]
    pick, tail_pick = picks_for(info, RING[:7])
    tail = jnp.concatenate([block[512:528, :] for block in blocks], axis=0)
    for g in range(8):
        main = jnp.concatenate([block[64 * g : 64 * g + 64, :] for block in blocks], axis=0)
        sums[g] = jnp.dot(pick, main, preferred_element_type=F32) + jnp.dot(
            tail_pick(g), tail, preferred_element_type=F32
        )


def embed_kernel(info, _, gain, early, low, high, out, sums):
    pick, tail_pick = picks_for(info, RING[7:])
    tail = high[512 - CUT : 528 - CUT, :]
    counts = info[:, 128:129]
    square = jnp.zeros((256, 1), F32)
    for g in range(8):
        main = low[64 * g : 64 * g + 64, :] if 64 * g < CUT else high[64 * g - CUT : 64 * g - CUT + 64, :]
        total = (
            early[g]
            + jnp.dot(pick, main, preferred_element_type=F32)
            + jnp.dot(tail_pick(g), tail, preferred_element_type=F32)
        )
        mean = total * gain[:, 512 * g : 512 * g + 512] / counts
        sums[g] = mean
        square += jnp.sum(mean * mean, axis=1, keepdims=True)
    scale = lax.rsqrt(square + 1e-06)
    for g in range(8):
        out[:, 512 * g : 512 * g + 512] = (sums[g] * scale).astype(BF)


def gather(info, blocks):
    vmem = pl.BlockSpec(memory_space=pltpu.VMEM)
    return pl.pallas_call(
        gather_kernel,
        out_shape=jax.ShapeDtypeStruct((8, 256, 512), F32),
        in_specs=[vmem] * 8,
        out_specs=vmem,
        compiler_params=pltpu.CompilerParams(vmem_limit_bytes=16 << 20),
        cost_estimate=pl.CostEstimate(
            flops=2 * 256 * 560 * 4096, bytes_accessed=6 << 20, transcendentals=0
        ),
    )(info, *blocks)


def embed(info, token, gain, early, low, high):
    vmem = pl.BlockSpec(memory_space=pltpu.VMEM)
    return pl.pallas_call(
        embed_kernel,
        out_shape=jax.ShapeDtypeStruct((256, 4096), BF),
        in_specs=[vmem] * 6,
        out_specs=vmem,
        scratch_shapes=[pltpu.VMEM((8, 256, 512), F32)],
        compiler_params=pltpu.CompilerParams(vmem_limit_bytes=16 << 20),
        cost_estimate=pl.CostEstimate(
            flops=2 * 256 * 80 * 4096, bytes_accessed=6 << 20, transcendentals=0
        ),
    )(info, token, gain, early, low, high)


def owned_kernel(owner, passages, out):
    hold = (owner[...] == lax.axis_index("seq")).astype(jnp.int32)
    segs = owner.shape[1]
    line = lax.broadcasted_iota(jnp.int32, (segs, segs), 0)
    lane = lax.broadcasted_iota(jnp.int32, (segs, segs), 1)
    rank = jnp.sum(jnp.where(line < lane, column(hold), 0), axis=0, keepdims=True)
    slot = lax.broadcasted_iota(jnp.int32, (out.shape[0], segs), 0)
    pick = jnp.where((rank == slot) & (hold == 1), 1.0, 0.0).astype(BF)
    out[...] = jnp.dot(pick, passages[...], preferred_element_type=F32).astype(BF)


def owned(owner, passages):
    vmem = pl.BlockSpec(memory_space=pltpu.VMEM)
    return pl.pallas_call(
        owned_kernel,
        out_shape=jax.ShapeDtypeStruct((passages.shape[0] // NZ, passages.shape[1]), BF),
        in_specs=[vmem] * 2,
        out_specs=vmem,
        compiler_params=pltpu.CompilerParams(vmem_limit_bytes=16 << 20),
        cost_estimate=pl.CostEstimate(
            flops=2 * 32 * 256 * 4096, bytes_accessed=3 << 20, transcendentals=0
        ),
    )(owner, passages)


NEAR = (0, -1, 1, 2)


def query_block(refs, row, n, m):
    if m < 3:
        return refs[m][1024 * n + row : 1024 * n + row + 256, :]
    at = 1024 * (n % 2) + row
    return refs[3 + n // 2][at : at + 256, :]


def order_features(passages, ordered):
    x, y, core, _ = place()
    for n, u in enumerate(NEAR):
        for m, v in enumerate(NEAR):
            dx, dy = u + core * (v - u), v + core * (u - v)
            chip = lax.rem(x + dx + 4, 4) * 4 + lax.rem(y + dy + 4, 4)
            cols = pl.ds(pl.multiple_of(chip * 256, 256), 256)
            to = 256 * (n * 4 + m)
            ordered[:, to : to + 256] = passages[:, cols]


def picks_of(positive, row):
    core = lax.rem(lax.axis_index("dp"), NC)
    at = core * 8 + row // 128
    return jnp.concatenate(
        [column(positive[pl.ds(at, 1), :]), column(positive[pl.ds(at + 1, 1), :])], axis=0
    )


def lanes(*values):
    lane = lax.broadcasted_iota(jnp.int32, (256, 128), 1)
    out = jnp.zeros((256, 128), F32)
    for n, value in enumerate(values):
        out = jnp.where(lane == n, value, out)
    return out


NT = (((1,), (1,)), ((), ()))


def own_kernel(scale, positive, passages, *refs):
    q_refs, all_q, stats, ordered = refs[:5], refs[5], refs[6], refs[7]
    order_features(passages, ordered)
    ids = lax.axis_index("dp") * 256 + lax.broadcasted_iota(jnp.int32, (1, 256), 1)
    for row in (0, 256, 512, 768):
        q = jnp.concatenate(
            [query_block(q_refs, row, n, m) for n in range(4) for m in range(4)], axis=1
        )
        rows = slice(row, row + 256)
        all_q[rows, :] = q
        wq = q.astype(F32)
        factor = scale[...] * lax.rsqrt(jnp.sum(wq * wq, axis=1, keepdims=True) + 1e-06)
        scores = lax.dot_general(q, ordered[...], NT, preferred_element_type=F32) * factor
        hit = ids == picks_of(positive, row)
        chosen = jnp.sum(jnp.where(hit, scores, 0.0), axis=1, keepdims=True)
        top = jnp.max(scores, axis=1, keepdims=True)
        total = jnp.sum(jnp.exp(scores - top), axis=1, keepdims=True)
        stats[rows, :] = lanes(top, total, chosen, factor)


def other_kernel(positive, passages, all_q, early, out, ordered, stats):
    order_features(passages, ordered)
    dp = lax.axis_index("dp")
    first = (dp + along(lax.rem(dp, NC))) * 256
    ids = first + lax.broadcasted_iota(jnp.int32, (1, 256), 1)

    for row in (0, 256, 512, 768):
        rows = pl.ds(row, 256)
        have = early[rows, :]
        factor = have[:, 3:4]
        scores = lax.dot_general(all_q[rows, :], ordered[...], NT, preferred_element_type=F32)
        scores = scores * factor
        hit = ids == picks_of(positive, row)
        chosen = jnp.sum(jnp.where(hit, scores, 0.0), axis=1, keepdims=True) + have[:, 2:3]
        top = jnp.maximum(jnp.max(scores, axis=1, keepdims=True), have[:, 0:1])
        total = jnp.sum(jnp.exp(scores - top), axis=1, keepdims=True)
        total = total + have[:, 1:2] * jnp.exp(have[:, 0:1] - top)
        stats[rows, :] = lanes(top, total, chosen)
    out[...] = jnp.transpose(stats[...])[0:8, :]


def score(scale, positive, mine, other, blocks):
    vmem = pl.BlockSpec(memory_space=pltpu.VMEM)
    params = pltpu.CompilerParams(vmem_limit_bytes=24 << 20)
    cost = pl.CostEstimate(
        flops=2 * 1024 * 256 * 4096, bytes_accessed=1 << 20, transcendentals=1024 * 256
    )
    all_q, early = pl.pallas_call(
        own_kernel,
        out_shape=(
            jax.ShapeDtypeStruct((1024, 4096), BF),
            jax.ShapeDtypeStruct((1024, 128), F32),
        ),
        in_specs=[vmem] * 8,
        out_specs=(vmem, vmem),
        scratch_shapes=[pltpu.VMEM((256, 4096), BF)],
        compiler_params=params,
        cost_estimate=cost,
    )(scale.reshape(1, 1), positive, mine, *blocks)
    return pl.pallas_call(
        other_kernel,
        out_shape=jax.ShapeDtypeStruct((8, 1024), F32),
        in_specs=[vmem] * 4,
        out_specs=vmem,
        scratch_shapes=[pltpu.VMEM((256, 4096), BF), pltpu.VMEM((1024, 128), F32)],
        compiler_params=params,
        cost_estimate=cost,
    )(positive, other, all_q, early)


ANY = pl.BlockSpec(memory_space=pl.ANY)


def fence(token):
    return pl.pallas_call(
        lambda token, out: None,
        out_shape=jax.ShapeDtypeStruct(token.shape, token.dtype),
        in_specs=[ANY],
        out_specs=ANY,
        input_output_aliases={0: 0},
        compiler_params=pltpu.CompilerParams(vmem_limit_bytes=1 << 20),
        cost_estimate=pl.CostEstimate(flops=20 * 10**9, bytes_accessed=8192, transcendentals=0),
    )(token)


def copied(rows_out, cuts, *arrays):
    def kernel(*refs):
        ins, outs, sems = refs[: len(arrays)], refs[len(arrays) : -1], refs[-1]
        copies = [
            pltpu.make_async_copy(
                ins[i].at[pl.ds(at, rows)], outs[o].at[pl.ds(to, rows)], sems.at[n]
            )
            for n, (i, at, rows, o, to) in enumerate(cuts)
        ]
        for copy in copies:
            copy.start()
        for copy in copies:
            copy.wait()

    return pl.pallas_call(
        kernel,
        out_shape=tuple(jax.ShapeDtypeStruct((rows, arrays[0].shape[1]), BF) for rows in rows_out),
        in_specs=[ANY] * len(arrays),
        out_specs=(ANY,) * len(rows_out),
        scratch_shapes=[pltpu.SemaphoreType.DMA((len(cuts),))],
        compiler_params=pltpu.CompilerParams(vmem_limit_bytes=1 << 20),
        cost_estimate=pl.CostEstimate(flops=10**6, bytes_accessed=1 << 20, transcendentals=0),
    )(*arrays)


def merge(parts):
    top = parts[0][0]
    for p in parts[1:]:
        top = jnp.maximum(top, p[0])
    total = sum(p[1] * jnp.exp(p[0] - top) for p in parts)
    chosen = sum(p[2] for p in parts)
    return jnp.stack([top, total, chosen])


def per_device(hidden, gain, seg_start, owner, queries, positive, logit_scale):
    core = lax.axis_index("dp") % NC
    half = queries.shape[0] // 2

    own = lax.dynamic_slice_in_dim(queries, core * half, half)
    away = lax.dynamic_slice_in_dim(queries, (1 - core) * half, half)
    back = move(away, dc=1)
    block = jnp.where(
        core == 0, jnp.concatenate([own, back], 1), jnp.concatenate([back, own], 1)
    )
    packed, info, token = pool(seg_start, hidden)

    got = {("q", 0): block, ("f", 0): packed, ("b", 0): packed}
    last = []
    token = [token]

    def take(names, hold=False):
        keys = [*names, *(k for k in last if k not in names)]
        *tied, mark = barrier((*(got[k] for k in keys), token[0]))
        got.update(zip(keys, tied))
        token[0] = fence(mark) if hold else mark
        last[:] = names

    def step(*names):
        take([(stream, n - 1) for stream, n in names], hold=True)
        for stream, n in names:
            got[stream, n] = turn(got[stream, n - 1], 1 if stream == "f" else -1)

    take([("q", 0)], hold=True)
    got["+", 1], got["-", 1] = pass_on(got["q", 0], 0, 1), pass_on(got["q", 0], 0, -1)
    got["far", 1] = pass_on(got["q", 0], 0, 2)
    step(("f", 1), ("b", 1))
    take([("+", 1), ("-", 1), ("far", 1)], hold=True)
    cuts = [(n, 0, half, 0, half * n) for n in range(4)]
    (line,) = copied((4 * half,), cuts, block, got["+", 1], got["-", 1], got["far", 1])
    got["+", 3], got["-", 3] = pass_on(line, 1, 1), pass_on(line, 1, -1)
    step(("f", 2), ("b", 2))
    step(("f", 3), ("b", 3))
    take([("+", 3), ("-", 3)], hold=True)
    cuts = [(0, 0, 2 * half, 0, 0), (1, 2 * half, 2 * half, 1, 0)]
    up, down = copied((2 * half, 2 * half), cuts, got["+", 3], got["-", 3])
    got["+", 4], got["-", 4] = pass_on(up, 1, 1), pass_on(down, 1, -1)
    take([("f", 3), ("b", 3)])
    cuts = [(0, 0, CUT, 0, 0), (1, CUT, PACKED - CUT, 1, 0)]
    up, down = copied((CUT, PACKED - CUT), cuts, got["f", 3], got["b", 3])
    got["f", 4], got["b", 4] = turn(up, 1), turn(down, -1)

    early = gather(info, [packed, *(got[k, n] for n in (1, 2, 3) for k in "fb")])
    mine = embed(info, token[0], gain[None, :], early, got["f", 4], got["b", 4])
    late = [("+", 4), ("-", 4)]
    mine, *rest = barrier((mine, *(got[k] for k in late)))
    got.update(zip(late, rest))
    other = move(mine, dc=1)
    blocks = [line, *(got[k] for k in (("+", 3), ("-", 3), ("+", 4), ("-", 4)))]
    stats = score(logit_scale, positive.reshape(16, 128), mine, other, blocks)
    pooled = owned(owner, mine)

    stats = stats[:3]
    stats = merge([stats, move(stats, dx=1), move(stats, dx=-1), move(stats, dx=2)])
    stats, pooled = barrier((stats, pooled))
    stats = merge([stats, move(stats, dy=1), move(stats, dy=-1), move(stats, dy=2)])
    part = stats[2] - stats[0] - jnp.log(stats[1])
    rest = move(part, dc=1)
    log_prob = jnp.where(core == 0, jnp.concatenate([part, rest]), jnp.concatenate([rest, part]))
    return pooled, log_prob


def solution(mesh):
    in_specs = (
        P("dp", "seq", None),
        P(),
        P("dp", None),
        P("dp", None),
        P("seq", "dp"),
        P("seq"),
        P(),
    )
    out_specs = (P(("dp", "seq"), None), P("seq"))
    return jax.shard_map(
        per_device, mesh=mesh, in_specs=in_specs, out_specs=out_specs, check_vma=False
    )
```
